32 devices in a mesh: fsdp: 8 (over z, core), grp: 2 (over y), tp: 2 (over x).
Axes of the slice: x: 2, y: 2, z: 4, core: 2. Of those that a mesh axis runs over, the one named last changes fastest.
Arguments:
- learn_in: bfloat16 [2752, 4096], P('fsdp', 'grp'), may hold values from -6 to 6
- learn_cot: bfloat16 [2752, 4096], P('fsdp', 'grp'), may hold values from -0.109375 to 0.109375
- preact: bfloat16 [2752, 2, 1536], P('fsdp', None, 'tp'), may hold values from -6 to 6
- hidden_cot: bfloat16 [2752, 1536], P('fsdp', 'tp'), may hold values from -0.109375 to 0.109375
- master: float32 [2, 2048, 3, 1536], P('grp', 'fsdp', None, 'tp'), may hold values from -0.09375 to 0.09375
- moment: float32 [2, 2048, 3, 1536], P('grp', 'fsdp', None, 'tp'), may hold values from -4 to 4
- second: float32 [2, 2048, 3, 1536], P('grp', 'fsdp', None, 'tp'), may hold values from 0.05 to 1
- rollout_in: bfloat16 [8192, 4096], P(('fsdp', 'grp'), 'tp'), may hold values from -6 to 6
- routes: int32 [8192, 8], P(('fsdp', 'grp')), may hold values from 0 to 127, as said below
- route_weight: float32 [8192, 8], P(('fsdp', 'grp')), may hold values from 0.05 to 0.6
Outputs:
- master_new: float32 [2, 2048, 3, 1536], P('grp', 'fsdp', None, 'tp')
- moment_new: float32 [2, 2048, 3, 1536], P('grp', 'fsdp', None, 'tp')
- second_new: float32 [2, 2048, 3, 1536], P('grp', 'fsdp', None, 'tp')
- expert_out: bfloat16 [8192, 4096], P(('fsdp', 'grp'), 'tp')
The draws below stay inside these ranges and needn't reach their ends.
Inputs may be any that keep to these rules, and one draw needn't show every extreme that they name: `routes`: each row names 8 different experts. In each rollout group of 512 consecutive rows, expert 0 is named by at most 112 rows, and by exactly 112 rows in at least one group.
All inputs are finite; a program needn't handle non-finite values.
Results may differ from the reference program's by a relative error of at most 0.022.
Values may be sent and summed in bfloat16 or wider, within the bound.
No kernel may reach another device: no remote copies, remote signals or barrier semaphores. Data moves between devices by JAX's collectives and lax.ppermute only.
A program may use at most 128 MiB of HBM per device.

```python
import math
import jax
import jax.numpy as jnp
from jax import lax

D = 4096
FF = 1536
EXPERTS = 128
TOPK = 8
TOK_DEV = 344
ROWS_DEV = 512
CAP = 112
LEARN_TOKENS = 2752
GROUPS = 16
ROLL_ROWS = 8192
N_FSDP = 8
N_GRP = 2


def draw_routes(key, part):
    key = jax.random.fold_in(key, 7)
    subkeys = jax.random.split(key, 5)
    scores = jax.random.randint(subkeys[0], (ROLL_ROWS, EXPERTS - 1), 0, 1 << 20) * (EXPERTS - 1) + jnp.arange(EXPERTS - 1, dtype=jnp.int32)[None, :]
    picked_ids = jnp.argsort(scores, axis=1)[:, :TOPK].astype(jnp.int32) + 1
    group_loads = jax.random.randint(subkeys[1], (GROUPS,), CAP // 2, CAP + 1)
    fullest = jax.random.randint(subkeys[2], (), 0, GROUPS)
    group_loads = jnp.where(jnp.arange(GROUPS, dtype=jnp.int32) == fullest, CAP, group_loads)
    ranking_keys = jax.random.randint(subkeys[3], (GROUPS, ROWS_DEV), 0, 1 << 20) * ROWS_DEV + jnp.arange(ROWS_DEV, dtype=jnp.int32)[None, :]
    row_ranks = jnp.argsort(jnp.argsort(ranking_keys, axis=1), axis=1)
    chosen = (row_ranks < group_loads[:, None]).reshape(ROLL_ROWS)
    position = jax.random.randint(subkeys[4], (ROLL_ROWS,), 0, TOPK)
    at_slot = jnp.arange(TOPK, dtype=jnp.int32)[None, :] == position[:, None]
    return jnp.where(chosen[:, None] & at_slot, 0, picked_ids).astype(jnp.int32)


def with_spikes(result, stream_key, source, target, blocks, factor):
    def block_of(dim):
        return (jnp.arange(result.shape[dim]) // (result.shape[dim] // blocks)).reshape((-1,) + (1,) * (result.ndim - 1 - dim))

    one_side = jax.random.permutation(stream_key, blocks)[block_of(target)]
    second = (block_of(target) + blocks // 2) % blocks
    return jnp.where((block_of(source) == one_side) | (block_of(source) == second), factor * result, result)


def levels(own_key, extent, pieces, low, top_value):
    gain = 1.0
    for dim, blocks in pieces:
        heights = jax.random.uniform(jax.random.fold_in(jax.random.fold_in(own_key, 6), dim), (blocks,), jnp.float32, low / len(pieces), top_value / len(pieces))
        gain = gain * jnp.repeat(jnp.exp(heights), extent[dim] // blocks).reshape((-1,) + (1,) * (len(extent) - 1 - dim))
    return gain


def gaussian(stream_key, extent, scale, limit, cuts=(), kind=jnp.bfloat16):
    factor_of = levels(stream_key, extent, cuts, -0.22, 0.18) if cuts else 1.0
    entries = jax.random.normal(stream_key, extent, jnp.float32) * scale * factor_of
    return jnp.minimum(jnp.maximum(entries, -limit), limit).astype(kind)


def noise_with(stream_key, shape, width, limit, cuts, heavy, kind=jnp.bfloat16):
    values = width * jax.random.normal(stream_key, shape, jnp.float32)
    if cuts:
        values = values * levels(stream_key, shape, cuts, -0.22, 0.18)
    return jnp.clip(with_spikes(values, jax.random.fold_in(stream_key, 3), *heavy), -limit, limit).astype(kind)


def setup_inputs(seed: int = 0) -> dict:
    key_list = jax.random.split(jax.random.key(seed), 11)
    return {
        "learn_in": noise_with(key_list[0], (LEARN_TOKENS, D), 1.0, 6.0, ((0, 8), (1, 2)), (0, 1, 8, 2.0)),
        "learn_cot": gaussian(key_list[1], (LEARN_TOKENS, D), (TOK_DEV * N_FSDP) ** -0.5, 0.109375, ((0, 8), (1, 2))),
        "preact": gaussian(key_list[2], (LEARN_TOKENS, 2, FF), 1.0, 6.0, ((0, 8), (2, 2))),
        "hidden_cot": gaussian(key_list[3], (LEARN_TOKENS, FF), (TOK_DEV * N_FSDP) ** -0.5, 0.109375, ((0, 8), (1, 2))),
        "master": gaussian(key_list[4], (N_GRP, D // N_GRP, 3, FF), D ** -0.5, 0.09375, ((0, 2), (1, 8), (3, 2)), jnp.float32),
        "moment": gaussian(key_list[5], (N_GRP, D // N_GRP, 3, FF), 0.5, 4.0, ((0, 2), (1, 8), (3, 2)), jnp.float32),
        "second": jnp.clip(jnp.exp(math.log(1.0) - 2.9957323 * jax.random.uniform(key_list[6], (N_GRP, D // N_GRP, 3, FF), jnp.float32) ** levels(key_list[6], (N_GRP, D // N_GRP, 3, FF), ((0, 2), (1, 8), (3, 2)), -0.2, 0.2)), 0.05, 1.0),
        "rollout_in": gaussian(key_list[7], (ROLL_ROWS, D), 1.0, 6.0, ((0, 16), (1, 2))),
        "routes": draw_routes(jax.random.fold_in(key_list[10], 71), 0),
        "route_weight": jnp.clip(jnp.exp(math.log(0.6) - 2.4849067 * jax.random.uniform(key_list[9], (ROLL_ROWS, TOPK), jnp.float32) ** levels(key_list[9], (ROLL_ROWS, TOPK), ((0, 16),), -0.2, 0.2)), 0.05, 0.6),
    }


first_decay = 0.9
second_decay = 0.95
first_fix = 1.0 - 0.9 ** 10
second_fix = 1.0 - 0.95 ** 10
learn_rate = 0.002
weight_decay = 0.1
epsilon = 1e-08

def reference(learn_in, learn_cot, preact, hidden_cot, master, moment, second, rollout_in, routes, route_weight):
    gate_pre = preact[:, 0, :].astype(jnp.float32)
    up_pre = preact[:, 1, :].astype(jnp.float32)
    logistic = jax.nn.sigmoid(gate_pre)
    activated = gate_pre * logistic
    hidden_act = (activated * up_pre).astype(jnp.bfloat16)
    cotangent = hidden_cot.astype(jnp.float32)
    grad_gate = (cotangent * up_pre * logistic * (1.0 + gate_pre * (1.0 - logistic))).astype(jnp.bfloat16)
    grad_up = (cotangent * activated).astype(jnp.bfloat16)
    pre_grads = jnp.concatenate([grad_gate, grad_up], axis=1)
    in_blocks = learn_in.reshape(N_FSDP, TOK_DEV, D)
    cot_blocks = learn_cot.reshape(N_FSDP, TOK_DEV, D)
    pre_blocks = pre_grads.reshape(N_FSDP, TOK_DEV, 2 * FF)
    act_blocks = hidden_act.reshape(N_FSDP, TOK_DEV, FF)

    def add_block(running, members):
        in_block, cot_block, pre_block, act_block = members
        front = jnp.dot(in_block.T, pre_block, preferred_element_type=jnp.float32).reshape(D, 2, FF)
        back = jnp.dot(cot_block.T, act_block, preferred_element_type=jnp.float32)[:, None, :]
        rounded = lax.optimization_barrier(jnp.concatenate([front, back], axis=1).astype(jnp.bfloat16))
        return (running + rounded.astype(jnp.float32), None)
    summed, unused = lax.scan(add_block, jnp.zeros((D, 3, FF), jnp.float32), (in_blocks, cot_blocks, pre_blocks, act_blocks))
    grad = summed.reshape(N_GRP, D // N_GRP, 3, FF)
    moment_new = first_decay * moment + (1.0 - first_decay) * grad
    second_new = second_decay * second + (1.0 - second_decay) * grad * grad
    step_size = moment_new / first_fix / (jnp.sqrt(second_new / second_fix) + epsilon)
    master_new = master - learn_rate * (step_size + weight_decay * master)
    passed = master_new.astype(jnp.bfloat16).reshape(D, 3, FF)
    weight_in = passed[:, :2, :].reshape(D, 2 * FF)
    weight_down = passed[:, 2, :]

    def one_group(members):
        group_rows, group_ids, group_weights = members
        named = group_ids == 0
        chosen_row = jnp.any(named, axis=1)
        row_weight = lax.optimization_barrier(jnp.sum(jnp.where(named, group_weights, 0.0), axis=1))
        ranking = jnp.argsort(1 - chosen_row.astype(jnp.int32), stable=True)[:CAP]
        filled = jnp.sum(chosen_row.astype(jnp.int32))
        usable = jnp.arange(CAP, dtype=jnp.int32) < filled
        picked = group_rows[ranking]
        slot_rows = jnp.where(usable[:, None], picked, jnp.zeros_like(picked))
        slot_pre = jnp.dot(slot_rows, weight_in, preferred_element_type=jnp.float32).reshape(CAP, 2, FF)
        slot_hidden = (jax.nn.silu(slot_pre[:, 0, :]) * slot_pre[:, 1, :]).astype(jnp.bfloat16)
        slot_out = jnp.dot(slot_hidden, weight_down.T, preferred_element_type=jnp.float32)
        slot_of_row = jnp.clip(jnp.cumsum(chosen_row.astype(jnp.int32)) - 1, 0, CAP - 1)
        placed = row_weight[:, None] * slot_out[slot_of_row]
        return jnp.where(chosen_row[:, None], placed, jnp.zeros_like(placed)).astype(jnp.bfloat16)
    expert_out = lax.map(one_group, (rollout_in.reshape(GROUPS, ROWS_DEV, D), routes.reshape(GROUPS, ROWS_DEV, TOPK), route_weight.reshape(GROUPS, ROWS_DEV, TOPK)))
    return (master_new, moment_new, second_new, expert_out.reshape(ROLL_ROWS, D))
```

```python
import jax
import jax.numpy as jnp
from jax import lax
from jax.sharding import PartitionSpec as P

CAP = 112

first_decay = 0.9
second_decay = 0.95
first_fix = 1.0 - 0.9**10
second_fix = 1.0 - 0.95**10
learn_rate = 0.002
weight_decay = 0.1
epsilon = 1e-08

F32 = jnp.float32
BF16 = jnp.bfloat16
BY_TOKENS = (((0,), (0,)), ((), ()))
BY_LAST = (((1,), (1,)), ((), ()))

CORES = [(i, i ^ 1) for i in range(8)]
SIBLINGS = [(i, i ^ 2) for i in range(8)]
INWARD = [(0, 2), (1, 3), (6, 4), (7, 5)]
MIDDLE = [(2, 4), (3, 5), (4, 2), (5, 3)]
OUTWARD = [(2, 0), (3, 1), (4, 6), (5, 7)]
SWAP = [(0, 1), (1, 0)]


def activations(preact, hidden_cot):
    gate_pre = preact[:, 0, :].astype(F32)
    up_pre = preact[:, 1, :].astype(F32)
    logistic = jax.nn.sigmoid(gate_pre)
    activated = gate_pre * logistic
    hidden_act = (activated * up_pre).astype(BF16)
    cotangent = hidden_cot.astype(F32)
    grad_gate = (cotangent * up_pre * logistic * (1.0 + gate_pre * (1.0 - logistic))).astype(BF16)
    grad_up = (cotangent * activated).astype(BF16)
    return hidden_act, grad_gate, grad_up


def adam(master, moment, second, grad):
    moment_new = first_decay * moment + (1.0 - first_decay) * grad
    second_new = second_decay * second + (1.0 - second_decay) * grad * grad
    step_size = moment_new / first_fix / (jnp.sqrt(second_new / second_fix) + epsilon)
    master_new = master - learn_rate * (step_size + weight_decay * master)
    return master_new, moment_new, second_new


def slots(routes):
    named = routes == 0
    chosen_row = jnp.any(named, axis=1)
    slot_of_row = jnp.cumsum(chosen_row.astype(jnp.int32)) - 1
    place = jnp.arange(CAP, dtype=jnp.int32)[:, None] == slot_of_row[None, :]
    return named, (place & chosen_row[None, :]).astype(BF16)


def on_line(
    learn_in,
    learn_cot,
    preact,
    hidden_cot,
    master,
    moment,
    second,
    rollout_in,
    routes,
    route_weight,
):
    index = lax.axis_index("fsdp")
    core = index % 2
    chip = index // 2
    half = chip // 2
    odd = chip % 2
    grp = lax.axis_index("grp")
    tp = lax.axis_index("tp")
    tokens = learn_in.shape[0]
    width = preact.shape[2]
    rows = master.shape[1]

    def by_core(array):
        parts = array.reshape(array.shape[0], 4, 2, rows)
        keep = lax.dynamic_index_in_dim(parts, core, 2, False).reshape(-1, 4 * rows)
        give = lax.dynamic_index_in_dim(parts, 1 - core, 2, False).reshape(-1, 4 * rows)
        return keep, give

    def with_other_core(keep, give):
        return jnp.concatenate([keep, lax.ppermute(give, "fsdp", CORES)], axis=0)

    hidden_act, grad_gate, grad_up = activations(preact, hidden_cot)
    cot_cols = with_other_core(*by_core(learn_cot))
    in_cols = with_other_core(*by_core(learn_in))

    def reduce_line(cols, pre):
        far_cols = lax.dynamic_slice_in_dim(cols, (1 - half) * 2 * rows, 2 * rows, 1)
        near_cols = lax.dynamic_slice_in_dim(cols, half * 2 * rows, 2 * rows, 1)
        far = lax.dot_general(far_cols, pre, BY_TOKENS, preferred_element_type=F32)
        far = far.astype(BF16)
        from_outer = lax.ppermute(far, "fsdp", INWARD)
        far = (far.astype(F32) + from_outer.astype(F32)).astype(BF16)
        across = lax.ppermute(far, "fsdp", MIDDLE)
        near = lax.dot_general(near_cols, pre, BY_TOKENS, preferred_element_type=F32)
        near = near + across.astype(F32)
        sibling = lax.dynamic_slice_in_dim(near, (1 - odd) * rows, rows, 0).astype(BF16)
        own = lax.dynamic_slice_in_dim(near, odd * rows, rows, 0)
        return own + lax.ppermute(sibling, "fsdp", SIBLINGS).astype(F32)

    def gather_line(shard):
        other = lax.ppermute(shard, "fsdp", SIBLINGS)
        near = jnp.where(
            odd == 0, jnp.concatenate([shard, other]), jnp.concatenate([other, shard])
        )
        across = lax.ppermute(near, "fsdp", MIDDLE)
        far = across + lax.ppermute(across, "fsdp", OUTWARD)
        return near, far

    def updated(which, grad):
        return adam(master[0, :, which], moment[0, :, which], second[0, :, which], grad)

    named, place = slots(routes)
    picked = jnp.dot(place, rollout_in, preferred_element_type=F32).astype(BF16)
    keep, give = by_core(picked)
    both = jnp.stack([keep, lax.ppermute(give, "fsdp", CORES)])
    turned = lax.ppermute(both, ("grp", "tp"), [(0, 0), (1, 2), (2, 1), (3, 3)])
    beside = lax.ppermute(turned, "tp", SWAP)
    mine = jnp.where(tp == grp, turned, beside)
    theirs = jnp.where(tp == grp, beside, turned)
    slot_rows = jnp.concatenate([mine[0], theirs[0], mine[1], theirs[1]])
    near_rows = lax.dynamic_slice_in_dim(slot_rows, half * 2 * rows, 2 * rows, 1)
    far_rows = lax.dynamic_slice_in_dim(slot_rows, (1 - half) * 2 * rows, 2 * rows, 1)

    def slot_product(weights):
        near, far = weights
        product = jnp.dot(near_rows, near, preferred_element_type=F32) + jnp.dot(
            far_rows, far, preferred_element_type=F32
        )
        keep, give = product[: 2 * CAP], product[2 * CAP :]
        product = keep + lax.ppermute(give.astype(BF16), "fsdp", CORES).astype(F32)
        keep, give = product[:CAP], product[CAP:]
        return keep + lax.ppermute(give.astype(BF16), "grp", SWAP).astype(F32)

    act_both = with_other_core(hidden_act, hidden_act)
    down = updated(2, reduce_line(cot_cols, act_both))
    down_near, down_far = gather_line(down[0].astype(BF16))
    diagonal = grp == tp

    def plane(block):
        vertical = lax.ppermute(block, "grp", SWAP)
        first = jnp.where(diagonal, block, vertical)
        second = lax.ppermute(jnp.where(diagonal, vertical, block), "tp", SWAP)
        pair = jnp.concatenate([first, second], axis=1)
        return pair, lax.ppermute(pair, "fsdp", CORES)

    near_down = plane(down_near)
    far_down = plane(down_far)

    gate_both = with_other_core(grad_gate, grad_gate)
    gate = updated(0, reduce_line(in_cols, gate_both))
    up_both = with_other_core(grad_up, grad_up)
    up = updated(1, reduce_line(in_cols, up_both))
    gate_pre = slot_product(gather_line(gate[0].astype(BF16)))
    up_pre = slot_product(gather_line(up[0].astype(BF16)))

    hidden = (jax.nn.silu(gate_pre) * up_pre).astype(BF16)
    hidden = jnp.concatenate([hidden, lax.ppermute(hidden, "tp", SWAP)], axis=1)

    def out_pieces(blocks):
        own, other = blocks
        own = lax.dot_general(hidden, own, BY_LAST, preferred_element_type=F32).astype(BF16)
        other = lax.dot_general(hidden, other, BY_LAST, preferred_element_type=F32).astype(BF16)
        first = jnp.where(core == 0, own, other).reshape(CAP, 2, 1, rows)
        second = jnp.where(core == 0, other, own).reshape(CAP, 2, 1, rows)
        return jnp.concatenate([first, second], axis=2).reshape(CAP, 4 * rows)

    near_out = out_pieces(near_down)
    far_out = out_pieces(far_down)
    slot_out = jnp.where(
        half == 0,
        jnp.concatenate([near_out, far_out], axis=1),
        jnp.concatenate([far_out, near_out], axis=1),
    )
    row_weight = jnp.sum(jnp.where(named, route_weight, 0.0), axis=1)
    placed = lax.dot_general(place, slot_out, BY_TOKENS, preferred_element_type=F32)
    expert_out = (row_weight[:, None] * placed).astype(BF16)
    outs = [jnp.stack([gate[i], up[i], down[i]], axis=1)[None] for i in range(3)]
    return (*outs, expert_out)


def on_device(
    learn_in,
    learn_cot,
    preact,
    hidden_cot,
    master,
    moment,
    second,
    rollout_in,
    routes,
    route_weight,
):
    hidden_width = preact.shape[2]
    hidden_act, grad_gate, grad_up = activations(preact, hidden_cot)
    pre_grads = jnp.concatenate([grad_gate, grad_up], axis=1)
    front = lax.dot_general(
        learn_in, pre_grads, BY_TOKENS, preferred_element_type=F32
    ).reshape(master.shape[1] * lax.axis_size("fsdp"), 2, hidden_width)
    back = lax.dot_general(learn_cot, hidden_act, BY_TOKENS, preferred_element_type=F32)[:, None, :]
    grad = lax.psum_scatter(
        jnp.concatenate([front, back], axis=1).astype(BF16),
        "fsdp",
        scatter_dimension=0,
        tiled=True,
    ).astype(F32)[None]
    master_new, moment_new, second_new = adam(master, moment, second, grad)
    half_rows = lax.all_gather(master_new.astype(BF16), "fsdp", axis=1, tiled=True)
    passed = lax.all_gather(half_rows, "grp", axis=0, tiled=True).reshape(-1, 3, hidden_width)
    weight_in = passed[:, :2, :].reshape(-1, 2 * hidden_width)
    named, place = slots(routes)
    picked = jnp.dot(place, rollout_in, preferred_element_type=F32).astype(BF16)
    slot_rows = lax.all_gather(picked, "tp", axis=1, tiled=True)
    slot_pre = jnp.dot(slot_rows, weight_in, preferred_element_type=F32)
    slot_hidden = jax.nn.silu(slot_pre[:, :hidden_width]) * slot_pre[:, hidden_width:]
    partial_out = lax.dot_general(
        slot_hidden.astype(BF16), passed[:, 2, :], BY_LAST, preferred_element_type=F32
    )
    slot_out = lax.psum_scatter(
        partial_out.astype(BF16), "tp", scatter_dimension=1, tiled=True
    )
    row_weight = jnp.sum(jnp.where(named, route_weight, 0.0), axis=1)
    placed = lax.dot_general(place, slot_out, BY_TOKENS, preferred_element_type=F32)
    expert_out = (row_weight[:, None] * placed).astype(BF16)
    return (master_new, moment_new, second_new, expert_out)


def solution(mesh):
    in_specs = (
        P("fsdp", "grp"),
        P("fsdp", "grp"),
        P("fsdp", None, "tp"),
        P("fsdp", "tp"),
        P("grp", "fsdp", None, "tp"),
        P("grp", "fsdp", None, "tp"),
        P("grp", "fsdp", None, "tp"),
        P(("fsdp", "grp"), "tp"),
        P(("fsdp", "grp"), None),
        P(("fsdp", "grp"), None),
    )
    out_specs = (
        P("grp", "fsdp", None, "tp"),
        P("grp", "fsdp", None, "tp"),
        P("grp", "fsdp", None, "tp"),
        P(("fsdp", "grp"), "tp"),
    )
    small = (mesh.shape["fsdp"], mesh.shape["grp"], mesh.shape["tp"]) == (8, 2, 2)
    return jax.shard_map(
        on_line if small else on_device,
        mesh=mesh,
        in_specs=in_specs,
        out_specs=out_specs,
        check_vma=False,
    )
```

```python
import functools

import jax
import jax.numpy as jnp
from jax import lax
from jax.experimental import pallas as pl
from jax.experimental.pallas import tpu as pltpu
from jax.sharding import PartitionSpec as P

CAP = 112

first_decay = 0.9
second_decay = 0.95
first_fix = 1.0 - 0.9**10
second_fix = 1.0 - 0.95**10
learn_rate = 0.002
weight_decay = 0.1
epsilon = 1e-08

F32 = jnp.float32
BF16 = jnp.bfloat16
BY_TOKENS = (((0,), (0,)), ((), ()))
BY_LAST = (((1,), (1,)), ((), ()))

CORES = [(i, i ^ 1) for i in range(8)]
NEAR = [(i, i ^ 2) for i in range(8)]
FAR = [(i, i ^ 4) for i in range(8)]
SWAP = [(0, 1), (1, 0)]
TURN = [(0, 0), (1, 2), (2, 1), (3, 3)]
ROUND = [(0, 1), (1, 3), (3, 2), (2, 0)]


def activations(preact, hidden_cot):
    gate_pre = preact[:, 0, :].astype(F32)
    up_pre = preact[:, 1, :].astype(F32)
    logistic = jax.nn.sigmoid(gate_pre)
    activated = gate_pre * logistic
    hidden_act = (activated * up_pre).astype(BF16)
    cotangent = hidden_cot.astype(F32)
    grad_gate = (cotangent * up_pre * logistic * (1.0 + gate_pre * (1.0 - logistic))).astype(BF16)
    grad_up = (cotangent * activated).astype(BF16)
    return hidden_act, grad_gate, grad_up


def adam(master, moment, second, grad):
    moment_new = first_decay * moment + (1.0 - first_decay) * grad
    second_new = second_decay * second + (1.0 - second_decay) * grad * grad
    step_size = moment_new / first_fix / (jnp.sqrt(second_new / second_fix) + epsilon)
    master_new = master - learn_rate * (step_size + weight_decay * master)
    return master_new, moment_new, second_new


def slots(routes, route_weight):
    named = routes == 0
    chosen_row = jnp.any(named, axis=1)
    slot_of_row = jnp.cumsum(chosen_row.astype(jnp.int32)) - 1
    place = slot_of_row[:, None] == jnp.arange(CAP, dtype=jnp.int32)[None, :]
    place = (place & chosen_row[:, None]).astype(BF16)
    return place, jnp.sum(jnp.where(named, route_weight, 0.0), axis=1, keepdims=True)


def near_first(i):
    return i


def far_first(i):
    return ((i & 1) << 1) | (i >> 1)


def take_kernel(rows, order, place_ref, source, *targets):
    for t, target in enumerate(targets):
        core = place_ref[1] if t else 1 - place_ref[1]
        for i in range(4):
            block = 2 * (place_ref[0] ^ order(i)) + core
            start = pl.multiple_of(block * rows, rows)
            target[:, i * rows : (i + 1) * rows] = source[:, pl.ds(start, rows)]


def take_columns(array, rows, order, count, place):
    half = jax.ShapeDtypeStruct((array.shape[0], 4 * rows), array.dtype)
    return pl.pallas_call(
        functools.partial(take_kernel, rows, order),
        out_shape=(half,) * count,
        in_specs=[
            pl.BlockSpec(memory_space=pltpu.SMEM),
            pl.BlockSpec(memory_space=pltpu.VMEM),
        ],
        out_specs=(pl.BlockSpec(memory_space=pltpu.VMEM),) * count,
        cost_estimate=pl.CostEstimate(
            flops=0, bytes_accessed=count * array.size * 2, transcendentals=0
        ),
    )(place, array)


def product_kernel(place_ref, own, got, own_pre, got_pre, out):
    total = lax.dot_general(own[...], own_pre[...], BY_TOKENS, preferred_element_type=F32)
    total += lax.dot_general(got[...], got_pre[...], BY_TOKENS, preferred_element_type=F32)
    out[...] = total.astype(out.dtype)


def token_product(own, got, own_pre, got_pre, place, first, dtype):
    tokens, width = own_pre.shape
    rows = got.shape[1] // 4
    pre = pl.BlockSpec((tokens, width), lambda i, p: (0, 0))

    def own_block(i, p):
        return 0, 2 * (p[0] ^ far_first(first + i)) + p[1]

    return pl.pallas_call(
        product_kernel,
        out_shape=jax.ShapeDtypeStruct((2 * rows, width), dtype),
        grid_spec=pltpu.PrefetchScalarGridSpec(
            num_scalar_prefetch=1,
            grid=(2,),
            in_specs=[
                pl.BlockSpec((tokens, rows), own_block),
                pl.BlockSpec((tokens, rows), lambda i, p: (0, first + i)),
                pre,
                pre,
            ],
            out_specs=pl.BlockSpec((rows, width), lambda i, p: (i, 0)),
        ),
        compiler_params=pltpu.CompilerParams(vmem_limit_bytes=32 << 20),
        cost_estimate=pl.CostEstimate(
            flops=8 * tokens * rows * width,
            bytes_accessed=8 * tokens * (width + rows),
            transcendentals=0,
        ),
    )(place, own, got, own_pre, got_pre)


def spread_kernel(place_ref, slots, weight, values, out):
    rows = out.shape[1] // 8
    for i in range(8):
        unit = place_ref[0] ^ ((i >> 2) | ((i & 1) << 1))
        block = 2 * unit + (place_ref[1] ^ ((i >> 1) & 1))
        placed = jnp.dot(
            slots[...], values[:, i * rows : (i + 1) * rows], preferred_element_type=F32
        )
        start = pl.multiple_of(block * rows, rows)
        out[:, pl.ds(start, rows)] = (weight[...] * placed).astype(out.dtype)


def spread(values, slots, weight, place):
    count, width = slots.shape[0], values.shape[1]
    step = count // 4
    return pl.pallas_call(
        spread_kernel,
        out_shape=jax.ShapeDtypeStruct((count, width), BF16),
        grid_spec=pltpu.PrefetchScalarGridSpec(
            num_scalar_prefetch=1,
            grid=(4,),
            in_specs=[
                pl.BlockSpec((step, CAP), lambda i, p: (i, 0)),
                pl.BlockSpec((step, 1), lambda i, p: (i, 0)),
                pl.BlockSpec((CAP, width), lambda i, p: (0, 0)),
            ],
            out_specs=pl.BlockSpec((step, width), lambda i, p: (i, 0)),
        ),
        compiler_params=pltpu.CompilerParams(vmem_limit_bytes=32 << 20),
    )(place, slots, weight, values)


def on_line(
    learn_in,
    learn_cot,
    preact,
    hidden_cot,
    master,
    moment,
    second,
    rollout_in,
    routes,
    route_weight,
):
    index = lax.axis_index("fsdp")
    grp = lax.axis_index("grp")
    tp = lax.axis_index("tp")
    line = jnp.stack([index // 2, index % 2])
    rows = master.shape[1]
    width = preact.shape[2]
    cut = 2 * width // 3
    last = None

    def swap(block, pairs):
        return lax.ppermute(block, "fsdp", pairs)

    def step(array):
        nonlocal last
        if last is not None:
            array = lax.optimization_barrier((array, last))[0]
        last = array
        return array

    def given(own, got, pre, got_pre):
        return token_product(own, got, pre, got_pre, line, 2, BF16)

    def kept(own, got, pre, got_pre):
        return token_product(own, got, pre, got_pre, line, 0, F32)

    def pair_sum(own, other):
        total = own + other.astype(F32)
        return total[:rows], total[rows:].astype(BF16)

    def updated(which, span, own, other):
        return adam(
            master[0, :, which, span],
            moment[0, :, which, span],
            second[0, :, which, span],
            own + other.astype(F32),
        )

    hidden_act, grad_gate, grad_up = activations(preact, hidden_cot)
    (cot_give,) = take_columns(learn_cot, rows, far_first, 1, line)
    hidden_act = step(hidden_act)
    down_args = (learn_cot, swap(cot_give, CORES), hidden_act, swap(hidden_act, CORES))
    d_given = step(given(*down_args))
    d_got = swap(d_given, NEAR)

    place, weight = slots(routes, route_weight)
    picked = lax.dot_general(step(place), rollout_in, BY_TOKENS, preferred_element_type=F32)
    picked = step(picked.astype(BF16))
    row_give, row_keep = take_columns(picked, rows, near_first, 2, line)
    row_got = swap(step(row_give), CORES)
    (in_give,) = take_columns(step(learn_in), rows, far_first, 1, line)
    in_got = swap(step(in_give), CORES)
    grad_gate = step(grad_gate)
    gate_args = (learn_in, in_got, grad_gate, swap(grad_gate, CORES))
    here = step(jnp.stack([row_keep, row_got]))
    there = swap(here[..., 2 * rows :], FAR)
    g_given = step(given(*gate_args))
    d_kept = step(kept(*down_args))
    d_own, d_give = pair_sum(d_kept, d_got)
    d_give = step(d_give)
    d_across = swap(d_give, FAR)
    g_got = swap(step(g_given), NEAR)

    both = step(jnp.stack([here[..., : 2 * rows], there], axis=1))
    turned = lax.ppermute(both, ("grp", "tp"), TURN)
    other = lax.ppermute(both, ("grp", "tp"), ROUND)
    grad_up = step(grad_up)
    got_up = swap(grad_up, CORES)
    u_args = (learn_in, in_got, grad_up[:, :cut], got_up[:, :cut])
    v_args = (learn_in, in_got, grad_up[:, cut:], got_up[:, cut:])
    u_given = step(given(*u_args))
    g_kept = step(kept(*gate_args))
    whole = slice(None)
    d_all = updated(2, whole, d_own, d_across)
    d_shard = step(d_all[0].astype(BF16))
    d_other = swap(d_shard, FAR)
    g_own, g_give = pair_sum(g_kept, g_got)
    g_give = step(g_give)
    g_across = swap(g_give, FAR)
    u_got = swap(step(u_given), NEAR)

    mine = jnp.where(tp == grp, turned, other)
    theirs = jnp.where(tp == grp, other, turned)
    slot_rows = step(jnp.stack([mine, theirs], axis=1).reshape(-1, 2 * rows))
    v_given = step(given(*v_args))
    u_kept = step(kept(*u_args))
    v_kept = step(kept(*v_args))
    d_near = step(jnp.concatenate([d_shard, d_other]))
    vertical = lax.ppermute(d_near, "grp", SWAP)
    g_all = updated(0, whole, g_own, g_across)
    g_shard = step(g_all[0].astype(BF16))
    g_near = swap(g_shard, NEAR)
    u_own, u_give = pair_sum(u_kept, u_got)
    u_give = step(u_give)
    u_across = swap(u_give, FAR)
    v_got = swap(step(v_given), NEAR)

    diagonal = grp == tp
    first = jnp.where(diagonal, d_near, vertical)
    second_half = lax.ppermute(step(jnp.where(diagonal, vertical, d_near)), "tp", SWAP)

    def slot_product(shard, other):
        total = jnp.dot(slot_rows[:, :rows], shard, preferred_element_type=F32)
        return total + jnp.dot(slot_rows[:, rows:], other, preferred_element_type=F32)

    def fold(total, axis, pairs):
        keep, give = jnp.split(total, 2)
        return keep + lax.ppermute(step(give.astype(BF16)), axis, pairs).astype(F32)

    g_part = fold(slot_product(g_shard, g_near), "fsdp", CORES)
    u_all = updated(1, slice(0, cut), u_own, u_across)
    u_shard = step(u_all[0].astype(BF16))
    u_near = swap(u_shard, NEAR)
    v_own, v_give = pair_sum(v_kept, v_got)
    v_give = step(v_give)
    v_across = swap(v_give, FAR)
    g_part = fold(g_part, "grp", SWAP)
    v_all = updated(1, slice(cut, width), v_own, v_across)
    v_shard = step(v_all[0].astype(BF16))
    v_near = swap(v_shard, NEAR)
    gate_pre = fold(g_part, "fsdp", FAR)
    u_part = fold(slot_product(u_shard, u_near), "fsdp", CORES)
    u_part = fold(u_part, "grp", SWAP)
    v_part = fold(slot_product(v_shard, v_near), "fsdp", CORES)
    v_part = fold(v_part, "grp", SWAP)
    u_part = fold(u_part, "fsdp", FAR)
    v_part = fold(v_part, "fsdp", FAR)
    up_pre = jnp.concatenate([u_part, v_part], axis=1)
    down = jnp.concatenate([first, second_half], axis=1)
    down = jnp.concatenate([down, swap(down, CORES)])

    hidden = (jax.nn.silu(gate_pre) * up_pre).astype(BF16)
    near_hidden = swap(hidden, NEAR)
    hidden = jnp.concatenate([hidden, lax.ppermute(hidden, "tp", SWAP)], axis=1)
    near_hidden = jnp.concatenate([near_hidden, lax.ppermute(near_hidden, "tp", SWAP)], axis=1)
    near_out = lax.dot_general(near_hidden, down, BY_LAST, preferred_element_type=F32)
    near_out = swap(near_out.astype(BF16), NEAR)
    out = lax.dot_general(hidden, down, BY_LAST, preferred_element_type=F32).astype(BF16)
    slot_out = jnp.concatenate([out, near_out], axis=1)
    expert_out = spread(slot_out, place, weight, line)
    up_all = [jnp.concatenate([u_all[i], v_all[i]], axis=1) for i in range(3)]
    outs = [jnp.stack([g_all[i], up_all[i], d_all[i]], axis=1)[None] for i in range(3)]
    return (*outs, expert_out)


def on_device(
    learn_in,
    learn_cot,
    preact,
    hidden_cot,
    master,
    moment,
    second,
    rollout_in,
    routes,
    route_weight,
):
    hidden_width = preact.shape[2]
    hidden_act, grad_gate, grad_up = activations(preact, hidden_cot)
    pre_grads = jnp.concatenate([grad_gate, grad_up], axis=1)
    front = lax.dot_general(
        learn_in, pre_grads, BY_TOKENS, preferred_element_type=F32
    ).reshape(master.shape[1] * lax.axis_size("fsdp"), 2, hidden_width)
    back = lax.dot_general(learn_cot, hidden_act, BY_TOKENS, preferred_element_type=F32)[:, None, :]
    grad = lax.psum_scatter(
        jnp.concatenate([front, back], axis=1).astype(BF16),
        "fsdp",
        scatter_dimension=0,
        tiled=True,
    ).astype(F32)[None]
    master_new, moment_new, second_new = adam(master, moment, second, grad)
    half_rows = lax.all_gather(master_new.astype(BF16), "fsdp", axis=1, tiled=True)
    passed = lax.all_gather(half_rows, "grp", axis=0, tiled=True).reshape(-1, 3, hidden_width)
    weight_in = passed[:, :2, :].reshape(-1, 2 * hidden_width)
    place, weight = slots(routes, route_weight)
    picked = lax.dot_general(place, rollout_in, BY_TOKENS, preferred_element_type=F32).astype(BF16)
    slot_rows = lax.all_gather(picked, "tp", axis=1, tiled=True)
    slot_pre = jnp.dot(slot_rows, weight_in, preferred_element_type=F32)
    slot_hidden = jax.nn.silu(slot_pre[:, :hidden_width]) * slot_pre[:, hidden_width:]
    partial_out = lax.dot_general(
        slot_hidden.astype(BF16), passed[:, 2, :], BY_LAST, preferred_element_type=F32
    )
    slot_out = lax.psum_scatter(
        partial_out.astype(BF16), "tp", scatter_dimension=1, tiled=True
    )
    placed = jnp.dot(place, slot_out, preferred_element_type=F32)
    expert_out = (weight * placed).astype(BF16)
    return (master_new, moment_new, second_new, expert_out)


def solution(mesh):
    in_specs = (
        P("fsdp", "grp"),
        P("fsdp", "grp"),
        P("fsdp", None, "tp"),
        P("fsdp", "tp"),
        P("grp", "fsdp", None, "tp"),
        P("grp", "fsdp", None, "tp"),
        P("grp", "fsdp", None, "tp"),
        P(("fsdp", "grp"), "tp"),
        P(("fsdp", "grp"), None),
        P(("fsdp", "grp"), None),
    )
    out_specs = (
        P("grp", "fsdp", None, "tp"),
        P("grp", "fsdp", None, "tp"),
        P("grp", "fsdp", None, "tp"),
        P(("fsdp", "grp"), "tp"),
    )
    small = (mesh.shape["fsdp"], mesh.shape["grp"], mesh.shape["tp"]) == (8, 2, 2)
    return jax.shard_map(
        on_line if small else on_device,
        mesh=mesh,
        in_specs=in_specs,
        out_specs=out_specs,
        check_vma=False,
    )
```

```python
import functools

import jax
import jax.numpy as jnp
from jax import lax
from jax.experimental import pallas as pl
from jax.experimental.pallas import tpu as pltpu
from jax.sharding import PartitionSpec as P

CAP = 112

first_decay = 0.9
second_decay = 0.95
first_fix = 1.0 - 0.9**10
second_fix = 1.0 - 0.95**10
learn_rate = 0.002
weight_decay = 0.1
epsilon = 1e-08

F32 = jnp.float32
BF16 = jnp.bfloat16
SMALL = pl.CostEstimate(flops=0, bytes_accessed=0, transcendentals=0)
BY_TOKENS = (((0,), (0,)), ((), ()))
BY_LAST = (((1,), (1,)), ((), ()))

CORES = [(i, i ^ 1) for i in range(8)]
NEAR = [(i, i ^ 2) for i in range(8)]
FAR = [(i, i ^ 4) for i in range(8)]
SWAP = [(0, 1), (1, 0)]
NEAR_TURNED = [(i, i ^ 5) for i in range(16)]
TURN = [(0, 0), (1, 2), (2, 1), (3, 3)]
ROUND = [(0, 1), (1, 3), (3, 2), (2, 0)]


def activations(preact, hidden_cot):
    gate_pre = preact[:, 0, :].astype(F32)
    up_pre = preact[:, 1, :].astype(F32)
    logistic = jax.nn.sigmoid(gate_pre)
    activated = gate_pre * logistic
    hidden_act = (activated * up_pre).astype(BF16)
    cotangent = hidden_cot.astype(F32)
    grad_gate = (cotangent * up_pre * logistic * (1.0 + gate_pre * (1.0 - logistic))).astype(BF16)
    grad_up = (cotangent * activated).astype(BF16)
    return hidden_act, grad_gate, grad_up


def adam(master, moment, second, grad):
    moment_new = first_decay * moment + (1.0 - first_decay) * grad
    second_new = second_decay * second + (1.0 - second_decay) * grad * grad
    step_size = moment_new / first_fix / (jnp.sqrt(second_new / second_fix) + epsilon)
    master_new = master - learn_rate * (step_size + weight_decay * master)
    return master_new, moment_new, second_new


def slots(routes, route_weight):
    named = routes == 0
    chosen_row = jnp.any(named, axis=1)
    slot_of_row = jnp.cumsum(chosen_row.astype(jnp.int32)) - 1
    place = slot_of_row[:, None] == jnp.arange(CAP, dtype=jnp.int32)[None, :]
    place = (place & chosen_row[:, None]).astype(BF16)
    return place, jnp.sum(jnp.where(named, route_weight, 0.0), axis=1, keepdims=True)


def pick(place, rollout_in):
    return lax.dot_general(place, rollout_in, BY_TOKENS, preferred_element_type=F32).astype(BF16)


def near_first(i):
    return i


def far_first(i):
    return ((i & 1) << 1) | (i >> 1)


def take_kernel(rows, order, place_ref, source, *targets):
    for t, target in enumerate(targets):
        core = place_ref[1] if t else 1 - place_ref[1]
        for i in range(4):
            block = 2 * (place_ref[0] ^ order(i)) + core
            start = pl.multiple_of(block * rows, rows)
            target[:, i * rows : (i + 1) * rows] = source[:, pl.ds(start, rows)]


def take_columns(array, rows, order, count, place):
    half = jax.ShapeDtypeStruct((array.shape[0], 4 * rows), array.dtype)
    return pl.pallas_call(
        functools.partial(take_kernel, rows, order),
        out_shape=(half,) * count,
        in_specs=[
            pl.BlockSpec(memory_space=pltpu.SMEM),
            pl.BlockSpec(memory_space=pltpu.VMEM),
        ],
        out_specs=(pl.BlockSpec(memory_space=pltpu.VMEM),) * count,
        cost_estimate=SMALL,
    )(place, array)


def product_kernel(place_ref, *refs):
    own_pre, got_pre, *refs = refs
    count = len(refs) // 3
    for own, got, out in zip(refs[:count], refs[count : 2 * count], refs[2 * count :]):
        total = lax.dot_general(own[...], own_pre[...], BY_TOKENS, preferred_element_type=F32)
        total += lax.dot_general(got[...], got_pre[...], BY_TOKENS, preferred_element_type=F32)
        out[...] = total.astype(out.dtype)


def token_products(own, got, own_pre, got_pre, place, firsts, span, dtypes):
    tokens = own_pre.shape[0]
    rows = got.shape[1] // 4
    width = span.stop - span.start
    pre = pl.BlockSpec((tokens, width), lambda i, p: (0, span.start // width))

    def own_block(first):
        return lambda i, p: (0, 2 * (p[0] ^ far_first(first)) + p[1])

    def got_block(first):
        return lambda i, p: (0, first)

    blocks = [pl.BlockSpec((tokens, rows), own_block(first)) for first in firsts]
    blocks += [pl.BlockSpec((tokens, rows), got_block(first)) for first in firsts]
    outs = tuple(jax.ShapeDtypeStruct((rows, width), dtype) for dtype in dtypes)
    return pl.pallas_call(
        product_kernel,
        out_shape=outs,
        grid_spec=pltpu.PrefetchScalarGridSpec(
            num_scalar_prefetch=1,
            grid=(1,),
            in_specs=[pre, pre] + blocks,
            out_specs=tuple(pl.BlockSpec((rows, width), lambda i, p: (0, 0)) for _ in outs),
        ),
        compiler_params=pltpu.CompilerParams(vmem_limit_bytes=32 << 20),
        cost_estimate=SMALL,
    )(place, own_pre, got_pre, *[own] * len(firsts), *[got] * len(firsts))


def spread_kernel(place_ref, slots, weight, values, out):
    rows = out.shape[1] // 8
    for i in range(8):
        unit = place_ref[0] ^ ((i >> 2) | ((i & 1) << 1))
        block = 2 * unit + (place_ref[1] ^ ((i >> 1) & 1))
        placed = jnp.dot(
            slots[...], values[:, i * rows : (i + 1) * rows], preferred_element_type=F32
        )
        start = pl.multiple_of(block * rows, rows)
        out[:, pl.ds(start, rows)] = (weight[...] * placed).astype(out.dtype)


def spread(values, slots, weight, place):
    count, width = slots.shape[0], values.shape[1]
    step = count // 4
    return pl.pallas_call(
        spread_kernel,
        out_shape=jax.ShapeDtypeStruct((count, width), BF16),
        grid_spec=pltpu.PrefetchScalarGridSpec(
            num_scalar_prefetch=1,
            grid=(4,),
            in_specs=[
                pl.BlockSpec((step, CAP), lambda i, p: (i, 0)),
                pl.BlockSpec((step, 1), lambda i, p: (i, 0)),
                pl.BlockSpec((CAP, width), lambda i, p: (0, 0)),
            ],
            out_specs=pl.BlockSpec((step, width), lambda i, p: (i, 0)),
        ),
        compiler_params=pltpu.CompilerParams(vmem_limit_bytes=32 << 20),
        cost_estimate=SMALL,
    )(place, slots, weight, values)


def row_kernel(place_ref, picked, there, *targets):
    rows = picked.shape[1] // 8
    chip, core = place_ref[0], place_ref[1]
    for target, parity in zip(targets, (1 - core, core)):
        for i in range(2):
            unit = chip ^ i
            start = pl.multiple_of((2 * unit + parity) * rows, rows)
            target[0, :, i * rows : (i + 1) * rows] = picked[:, pl.ds(start, rows)]
            start = pl.multiple_of((2 * (unit & 1) + parity) * rows, rows)
            target[1, :, i * rows : (i + 1) * rows] = there[:, pl.ds(start, rows)]


def split_rows(picked, there, rows, place):
    shape = jax.ShapeDtypeStruct((2, CAP, 2 * rows), BF16)
    return pl.pallas_call(
        row_kernel,
        out_shape=(shape, shape),
        in_specs=[
            pl.BlockSpec(memory_space=pltpu.SMEM),
            pl.BlockSpec(memory_space=pltpu.VMEM),
            pl.BlockSpec(memory_space=pltpu.VMEM),
        ],
        out_specs=(pl.BlockSpec(memory_space=pltpu.VMEM),) * 2,
        cost_estimate=SMALL,
    )(place, picked, there)


def on_line(
    learn_in,
    learn_cot,
    preact,
    hidden_cot,
    master,
    moment,
    second,
    rollout_in,
    routes,
    route_weight,
):
    index = lax.axis_index("fsdp")
    grp = lax.axis_index("grp")
    tp = lax.axis_index("tp")
    line = jnp.stack([index // 2, index % 2])
    rows = master.shape[1]
    width = preact.shape[2]
    last = None

    def send(name, block, axis, pairs):
        with jax.named_scope(name):
            return lax.ppermute(block, axis, pairs)

    def step(work, *operands):
        nonlocal last
        if last is not None:
            operands = lax.optimization_barrier((*operands, last))[:-1]
        done = work(*operands)
        last = done[0] if isinstance(done, tuple) else done
        return done

    def mark(done):
        nonlocal last
        several = isinstance(done, tuple)
        done = done if several else (done,)
        if last is not None:
            done = lax.optimization_barrier((*done, last))[:-1]
        last = done[0]
        return done if several else done[0]

    def hold(array):
        return lax.optimization_barrier((array, last))[0]

    def wait(array):
        nonlocal last
        array, last = lax.optimization_barrier((array, last))
        return array

    diagonal = grp == tp

    whole = slice(0, width)

    def give(order, count):
        return lambda array: take_columns(array, rows, order, count, line)

    def token_sums(first, span, dtype):
        return lambda *args: token_products(*args, line, first, span, dtype)

    def given_sum(own, other):
        return (own + other.astype(F32)).astype(BF16)

    def update(which, span):
        def work(own, near, across):
            total = own + near.astype(F32) + across.astype(F32)
            old = [array[0, :, which, span] for array in (master, moment, second)]
            new = adam(*old, total)
            return (new[0].astype(BF16), *new)

        return work

    def activated(preact, hidden_cot):
        return activations(preact, hidden_cot)[0]

    def pre_grads(preact, hidden_cot):
        return activations(preact, hidden_cot)[1:]

    def far_rows(picked):
        return lax.dynamic_slice_in_dim(picked, (1 - index // 4) * 4 * rows, 4 * rows, 1)

    def take_rows(picked, there):
        return split_rows(picked, there, rows, line)

    def both_cores(keep, got):
        return jnp.stack([keep, got])

    def plane_rows(turned, other):
        mine = jnp.where(diagonal, turned, other)
        theirs = jnp.where(diagonal, other, turned)
        by_grp, by_chip = jnp.stack([mine, theirs], axis=1), jnp.stack([mine, theirs], axis=2)
        return by_grp.reshape(-1, 2 * rows), by_chip.reshape(-1, 2 * rows)

    def joined(*blocks):
        return jnp.concatenate(blocks)

    def relayed(block, vertical):
        return jnp.where(diagonal, vertical, block)

    def plane_weights(*blocks):
        halves = [
            jnp.concatenate([jnp.where(diagonal, block, vertical), horizontal], axis=1)
            for block, vertical, horizontal in (blocks[:3], blocks[3:])
        ]
        return jnp.concatenate(halves)

    def stacked(*news):
        return tuple(jnp.stack(news[i::3], axis=1)[None] for i in range(3))

    def slot_product(slot_rows, left, right):
        total = jnp.dot(slot_rows[:, :rows], left, preferred_element_type=F32)
        total += jnp.dot(slot_rows[:, rows:], right, preferred_element_type=F32)
        keep, give = jnp.split(total, 2)
        return give.astype(BF16), keep

    def folded(kept, got):
        keep, give = jnp.split(kept + got.astype(F32), 2)
        return give.astype(BF16), keep

    def activate(*parts):
        sums = [kept + got.astype(F32) for kept, got in zip(parts[::2], parts[1::2])]
        up = jnp.concatenate(sums[1:], axis=1)
        return (jax.nn.silu(sums[0]) * up).astype(BF16)

    def down_product(left, right, near, far):
        slots = jnp.concatenate([left, right], axis=1)
        down = jnp.concatenate([near, far])
        return lax.dot_general(slots, down, BY_LAST, preferred_element_type=F32).astype(BF16)

    (cot_give,) = mark(give(far_first, 1)(learn_cot))
    cot_got = send("cot_got", cot_give, "fsdp", CORES)
    act = mark(activated(preact, hidden_cot))
    act_got = send("act_got", act, "fsdp", CORES)
    (d_gb,) = mark(token_sums((3,), whole, (BF16,))(learn_cot, cot_got, act, act_got))
    d_b = send("d_b", d_gb, "fsdp", NEAR)
    place, weight = mark(slots(routes, route_weight))
    picked = mark(pick(place, rollout_in))
    picked_far = mark(far_rows(picked))
    there = send("there", picked_far, "fsdp", FAR)
    (in_give,) = mark(give(far_first, 1)(learn_in))
    in_got = send("in_got", in_give, "fsdp", CORES)
    gate, up = mark(pre_grads(preact, hidden_cot))
    gate_got = send("gate_got", gate, "fsdp", CORES)
    up_got = send("up_got", up, "fsdp", CORES)
    g_gb, g_kb = mark(token_sums((3, 1), whole, (BF16, F32))(learn_in, in_got, gate, gate_got))
    d_ga, d_ka = mark(token_sums((2, 0), whole, (BF16, F32))(learn_cot, cot_got, act, act_got))
    d_a = send("d_a", d_ga, "fsdp", NEAR)
    g_b = send("g_b", g_gb, "fsdp", NEAR)
    (d_kb,) = mark(token_sums((1,), whole, (F32,))(learn_cot, cot_got, act, act_got))
    g_ga, g_ka = mark(token_sums((2, 0), whole, (BF16, F32))(learn_in, in_got, gate, gate_got))
    g_a = send("g_a", g_ga, "fsdp", NEAR)
    d_x = mark(given_sum(d_kb, d_b))
    d_across = send("d_across", d_x, "fsdp", FAR)
    g_x = mark(given_sum(g_kb, g_b))
    g_across = send("g_across", g_x, "fsdp", FAR)
    row_give, row_keep = mark(take_rows(picked, there))
    row_got = send("row_got", row_give, "fsdp", CORES)
    u_gb, u_kb = mark(token_sums((3, 1), whole, (BF16, F32))(learn_in, in_got, up, up_got))
    u_b = send("u_b", u_gb, "fsdp", NEAR)
    both = mark(both_cores(row_keep, row_got))
    turned = send("turned", both, ("grp", "tp"), TURN)
    rotated = send("rotated", both, ("grp", "tp"), ROUND)
    d_shard, *d_all = mark(update(2, whole)(d_ka, d_a, d_across))
    d_other = send("d_other", d_shard, "fsdp", FAR)
    vert_z = send("vert_z", d_shard, "grp", SWAP)
    g_shard, *g_all = mark(update(0, whole)(g_ka, g_a, g_across))
    g_near = send("g_near", g_shard, "fsdp", NEAR)
    u_x = mark(given_sum(u_kb, u_b))
    u_across = send("u_across", u_x, "fsdp", FAR)
    u_ga, u_ka = mark(token_sums((2, 0), whole, (BF16, F32))(learn_in, in_got, up, up_got))
    u_a = send("u_a", u_ga, "fsdp", NEAR)
    relay_z = mark(relayed(d_shard, vert_z))
    hori_z = send("hori_z", relay_z, "tp", SWAP)
    slot_rows, slot_rows_g = mark(plane_rows(turned, rotated))
    g_core, g_half = mark(slot_product(slot_rows_g, g_shard, g_near))
    g_core_got = send("g_core_got", g_core, "fsdp", CORES)
    g_far, g_quarter = mark(folded(g_half, g_core_got))
    g_far_got = send("g_far_got", g_far, "fsdp", FAR)
    u_shard, *u_all = mark(update(1, whole)(u_ka, u_a, u_across))
    u_near = send("u_near", u_shard, "fsdp", NEAR)
    d_other = wait(d_other)
    vert_f = send("vert_f", hold(d_other), "grp", SWAP)
    master_new, moment_new, second_new = mark(stacked(*g_all, *u_all, *d_all))
    hori_z = wait(hori_z)
    u_core, u_half = step(slot_product, slot_rows, u_shard, u_near)
    u_core_got = send("u_core_got", u_core, "fsdp", CORES)
    u_grp, u_quarter = step(folded, u_half, u_core_got)
    u_grp_got = send("u_grp_got", u_grp, "grp", SWAP)
    relay_f = step(relayed, d_other, vert_f)
    hori_f = send("hori_f", relay_f, "tp", SWAP)
    u_far, u_sum = step(folded, u_quarter, u_grp_got)
    u_far_got = send("u_far_got", u_far, "fsdp", FAR)
    g_grp, g_sum = step(folded, g_quarter, g_far_got)
    g_grp_got = send("g_grp_got", g_grp, "grp", SWAP)
    down = step(plane_weights, d_shard, vert_z, hori_z, d_other, vert_f, hori_f)
    down_got = send("down_got", down, "fsdp", CORES)
    hidden = mark(activate(g_sum, g_grp_got, u_sum, u_far_got))
    near_hidden = send("near_hidden", hidden, "fsdp", NEAR)
    near_turned = send("near_turned", hidden, ("fsdp", "tp"), NEAR_TURNED)
    beside = send("beside", hidden, "tp", SWAP)
    near_out = mark(down_product(near_hidden, near_turned, down, down_got))
    near_out_got = send("near_out_got", near_out, "fsdp", NEAR)
    out = mark(down_product(hidden, beside, down, down_got))

    slot_out = jnp.concatenate([out, near_out_got], axis=1)
    expert_out = spread(slot_out, place, weight, line)
    return (master_new, moment_new, second_new, expert_out)


def on_device(
    learn_in,
    learn_cot,
    preact,
    hidden_cot,
    master,
    moment,
    second,
    rollout_in,
    routes,
    route_weight,
):
    hidden_width = preact.shape[2]
    hidden_act, grad_gate, grad_up = activations(preact, hidden_cot)
    pre_grads = jnp.concatenate([grad_gate, grad_up], axis=1)
    front = lax.dot_general(
        learn_in, pre_grads, BY_TOKENS, preferred_element_type=F32
    ).reshape(master.shape[1] * lax.axis_size("fsdp"), 2, hidden_width)
    back = lax.dot_general(learn_cot, hidden_act, BY_TOKENS, preferred_element_type=F32)[:, None, :]
    grad = lax.psum_scatter(
        jnp.concatenate([front, back], axis=1).astype(BF16),
        "fsdp",
        scatter_dimension=0,
        tiled=True,
    ).astype(F32)[None]
    master_new, moment_new, second_new = adam(master, moment, second, grad)
    half_rows = lax.all_gather(master_new.astype(BF16), "fsdp", axis=1, tiled=True)
    passed = lax.all_gather(half_rows, "grp", axis=0, tiled=True).reshape(-1, 3, hidden_width)
    weight_in = passed[:, :2, :].reshape(-1, 2 * hidden_width)
    place, weight = slots(routes, route_weight)
    slot_rows = lax.all_gather(pick(place, rollout_in), "tp", axis=1, tiled=True)
    slot_pre = jnp.dot(slot_rows, weight_in, preferred_element_type=F32)
    slot_hidden = jax.nn.silu(slot_pre[:, :hidden_width]) * slot_pre[:, hidden_width:]
    partial_out = lax.dot_general(
        slot_hidden.astype(BF16), passed[:, 2, :], BY_LAST, preferred_element_type=F32
    )
    slot_out = lax.psum_scatter(
        partial_out.astype(BF16), "tp", scatter_dimension=1, tiled=True
    )
    placed = jnp.dot(place, slot_out, preferred_element_type=F32)
    expert_out = (weight * placed).astype(BF16)
    return (master_new, moment_new, second_new, expert_out)


def solution(mesh):
    in_specs = (
        P("fsdp", "grp"),
        P("fsdp", "grp"),
        P("fsdp", None, "tp"),
        P("fsdp", "tp"),
        P("grp", "fsdp", None, "tp"),
        P("grp", "fsdp", None, "tp"),
        P("grp", "fsdp", None, "tp"),
        P(("fsdp", "grp"), "tp"),
        P(("fsdp", "grp"), None),
        P(("fsdp", "grp"), None),
    )
    out_specs = (
        P("grp", "fsdp", None, "tp"),
        P("grp", "fsdp", None, "tp"),
        P("grp", "fsdp", None, "tp"),
        P(("fsdp", "grp"), "tp"),
    )
    small = (mesh.shape["fsdp"], mesh.shape["grp"], mesh.shape["tp"]) == (8, 2, 2)
    return jax.shard_map(
        on_line if small else on_device,
        mesh=mesh,
        in_specs=in_specs,
        out_specs=out_specs,
        check_vma=False,
    )
```

```python
import functools

import jax
import jax.numpy as jnp
from jax import lax
from jax.experimental import pallas as pl
from jax.experimental.pallas import tpu as pltpu
from jax.sharding import PartitionSpec as P

CAP = 112

first_decay = 0.9
second_decay = 0.95
first_fix = 1.0 - 0.9**10
second_fix = 1.0 - 0.95**10
learn_rate = 0.002
weight_decay = 0.1
epsilon = 1e-08

F32 = jnp.float32
BF16 = jnp.bfloat16
SMALL = pl.CostEstimate(flops=0, bytes_accessed=0, transcendentals=0)
BY_TOKENS = (((0,), (0,)), ((), ()))
BY_LAST = (((1,), (1,)), ((), ()))

CORES = [(i, i ^ 1) for i in range(8)]
NEAR = [(i, i ^ 2) for i in range(8)]
FAR = [(i, i ^ 4) for i in range(8)]
SWAP = [(0, 1), (1, 0)]
NEAR_TURNED = [(i, i ^ 5) for i in range(16)]
TURN = [(0, 0), (1, 2), (2, 1), (3, 3)]
ROUND = [(0, 1), (1, 3), (3, 2), (2, 0)]


def activations(preact, hidden_cot):
    gate_pre = preact[:, 0, :].astype(F32)
    up_pre = preact[:, 1, :].astype(F32)
    logistic = jax.nn.sigmoid(gate_pre)
    activated = gate_pre * logistic
    hidden_act = (activated * up_pre).astype(BF16)
    cotangent = hidden_cot.astype(F32)
    grad_gate = (cotangent * up_pre * logistic * (1.0 + gate_pre * (1.0 - logistic))).astype(BF16)
    grad_up = (cotangent * activated).astype(BF16)
    return hidden_act, grad_gate, grad_up


def adam(master, moment, second, grad):
    moment_new = first_decay * moment + (1.0 - first_decay) * grad
    second_new = second_decay * second + (1.0 - second_decay) * grad * grad
    step_size = moment_new / first_fix / (jnp.sqrt(second_new / second_fix) + epsilon)
    master_new = master - learn_rate * (step_size + weight_decay * master)
    return master_new, moment_new, second_new


def slots(routes, route_weight):
    named = routes == 0
    chosen_row = jnp.any(named, axis=1)
    slot_of_row = jnp.cumsum(chosen_row.astype(jnp.int32)) - 1
    place = slot_of_row[:, None] == jnp.arange(CAP, dtype=jnp.int32)[None, :]
    place = (place & chosen_row[:, None]).astype(BF16)
    return place, jnp.sum(jnp.where(named, route_weight, 0.0), axis=1, keepdims=True)


def pick(place, rollout_in):
    return lax.dot_general(place, rollout_in, BY_TOKENS, preferred_element_type=F32).astype(BF16)


def near_first(i):
    return i


def far_first(i):
    return ((i & 1) << 1) | (i >> 1)


def take_kernel(rows, order, place_ref, source, *targets):
    for t, target in enumerate(targets):
        core = place_ref[1] if t else 1 - place_ref[1]
        for i in range(4):
            block = 2 * (place_ref[0] ^ order(i)) + core
            start = pl.multiple_of(block * rows, rows)
            target[:, i * rows : (i + 1) * rows] = source[:, pl.ds(start, rows)]


def take_columns(array, rows, order, count, place):
    half = jax.ShapeDtypeStruct((array.shape[0], 4 * rows), array.dtype)
    return pl.pallas_call(
        functools.partial(take_kernel, rows, order),
        out_shape=(half,) * count,
        in_specs=[
            pl.BlockSpec(memory_space=pltpu.SMEM),
            pl.BlockSpec(memory_space=pltpu.VMEM),
        ],
        out_specs=(pl.BlockSpec(memory_space=pltpu.VMEM),) * count,
        cost_estimate=SMALL,
    )(place, array)


def product_kernel(place_ref, *refs):
    own_pre, got_pre, *refs = refs
    count = len(refs) // 3
    for own, got, out in zip(refs[:count], refs[count : 2 * count], refs[2 * count :]):
        total = lax.dot_general(own[...], own_pre[...], BY_TOKENS, preferred_element_type=F32)
        total += lax.dot_general(got[...], got_pre[...], BY_TOKENS, preferred_element_type=F32)
        out[...] = total.astype(out.dtype)


def token_products(own, got, own_pre, got_pre, place, firsts, span, dtypes):
    tokens = own_pre.shape[0]
    rows = got.shape[1] // 4
    width = span.stop - span.start
    pre = pl.BlockSpec((tokens, width), lambda i, p: (0, span.start // width))

    def own_block(first):
        return lambda i, p: (0, 2 * (p[0] ^ far_first(first)) + p[1])

    def got_block(first):
        return lambda i, p: (0, first)

    blocks = [pl.BlockSpec((tokens, rows), own_block(first)) for first in firsts]
    blocks += [pl.BlockSpec((tokens, rows), got_block(first)) for first in firsts]
    outs = tuple(jax.ShapeDtypeStruct((rows, width), dtype) for dtype in dtypes)
    return pl.pallas_call(
        product_kernel,
        out_shape=outs,
        grid_spec=pltpu.PrefetchScalarGridSpec(
            num_scalar_prefetch=1,
            grid=(1,),
            in_specs=[pre, pre] + blocks,
            out_specs=tuple(pl.BlockSpec((rows, width), lambda i, p: (0, 0)) for _ in outs),
        ),
        compiler_params=pltpu.CompilerParams(vmem_limit_bytes=32 << 20),
        cost_estimate=SMALL,
    )(place, own_pre, got_pre, *[own] * len(firsts), *[got] * len(firsts))


def spread_kernel(place_ref, slots, weight, values, out):
    rows = out.shape[1] // 8
    for i in range(8):
        unit = place_ref[0] ^ ((i >> 2) | ((i & 1) << 1))
        block = 2 * unit + (place_ref[1] ^ ((i >> 1) & 1))
        placed = jnp.dot(
            slots[...], values[:, i * rows : (i + 1) * rows], preferred_element_type=F32
        )
        start = pl.multiple_of(block * rows, rows)
        out[:, pl.ds(start, rows)] = (weight[...] * placed).astype(out.dtype)


def spread(values, slots, weight, place):
    count, width = slots.shape[0], values.shape[1]
    step = count // 2
    return pl.pallas_call(
        spread_kernel,
        out_shape=jax.ShapeDtypeStruct((count, width), BF16),
        grid_spec=pltpu.PrefetchScalarGridSpec(
            num_scalar_prefetch=1,
            grid=(2,),
            in_specs=[
                pl.BlockSpec((step, CAP), lambda i, p: (i, 0)),
                pl.BlockSpec((step, 1), lambda i, p: (i, 0)),
                pl.BlockSpec((CAP, width), lambda i, p: (0, 0)),
            ],
            out_specs=pl.BlockSpec((step, width), lambda i, p: (i, 0)),
        ),
        compiler_params=pltpu.CompilerParams(vmem_limit_bytes=32 << 20),
        cost_estimate=SMALL,
    )(place, slots, weight, values)


def row_kernel(place_ref, picked, there, *targets):
    rows = picked.shape[1] // 8
    chip, core = place_ref[0], place_ref[1]
    for target, parity in zip(targets, (1 - core, core)):
        for i in range(2):
            unit = chip ^ i
            start = pl.multiple_of((2 * unit + parity) * rows, rows)
            target[0, :, i * rows : (i + 1) * rows] = picked[:, pl.ds(start, rows)]
            start = pl.multiple_of((2 * (unit & 1) + parity) * rows, rows)
            target[1, :, i * rows : (i + 1) * rows] = there[:, pl.ds(start, rows)]


def split_rows(picked, there, rows, place):
    shape = jax.ShapeDtypeStruct((2, CAP, 2 * rows), BF16)
    return pl.pallas_call(
        row_kernel,
        out_shape=(shape, shape),
        in_specs=[
            pl.BlockSpec(memory_space=pltpu.SMEM),
            pl.BlockSpec(memory_space=pltpu.VMEM),
            pl.BlockSpec(memory_space=pltpu.VMEM),
        ],
        out_specs=(pl.BlockSpec(memory_space=pltpu.VMEM),) * 2,
        cost_estimate=SMALL,
    )(place, picked, there)


def on_line(
    learn_in,
    learn_cot,
    preact,
    hidden_cot,
    master,
    moment,
    second,
    rollout_in,
    routes,
    route_weight,
):
    index = lax.axis_index("fsdp")
    grp = lax.axis_index("grp")
    tp = lax.axis_index("tp")
    line = jnp.stack([index // 2, index % 2])
    rows = master.shape[1]
    width = preact.shape[2]
    last = None

    def send(name, block, axis, pairs):
        with jax.named_scope(name):
            return lax.ppermute(block, axis, pairs)

    def step(work, *operands):
        nonlocal last
        if last is not None:
            operands = lax.optimization_barrier((*operands, last))[:-1]
        done = work(*operands)
        last = done[0] if isinstance(done, tuple) else done
        return done

    def mark(done):
        nonlocal last
        several = isinstance(done, tuple)
        done = done if several else (done,)
        if last is not None:
            done = lax.optimization_barrier((*done, last))[:-1]
        last = done[0]
        return done if several else done[0]

    def hold(array):
        return lax.optimization_barrier((array, last))[0]

    def wait(array):
        nonlocal last
        array, last = lax.optimization_barrier((array, last))
        return array

    diagonal = grp == tp

    whole = slice(0, width)

    def give(order, count):
        return lambda array: take_columns(array, rows, order, count, line)

    def token_sums(first, span, dtype):
        return lambda *args: token_products(*args, line, first, span, dtype)

    def given_sum(own, other):
        return (own + other.astype(F32)).astype(BF16)

    def update(which, span):
        def work(own, near, across):
            total = own + near.astype(F32) + across.astype(F32)
            old = [array[0, :, which, span] for array in (master, moment, second)]
            new = adam(*old, total)
            return (new[0].astype(BF16), *new)

        return work

    def activated(preact, hidden_cot):
        return activations(preact, hidden_cot)[0]

    def pre_grads(preact, hidden_cot):
        return activations(preact, hidden_cot)[1:]

    def far_rows(picked):
        return lax.dynamic_slice_in_dim(picked, (1 - index // 4) * 4 * rows, 4 * rows, 1)

    def take_rows(picked, there):
        return split_rows(picked, there, rows, line)

    def both_cores(keep, got):
        return jnp.stack([keep, got])

    def plane_rows(turned, other):
        mine = jnp.where(diagonal, turned, other)
        theirs = jnp.where(diagonal, other, turned)
        by_grp, by_chip = jnp.stack([mine, theirs], axis=1), jnp.stack([mine, theirs], axis=2)
        return by_grp.reshape(-1, 2 * rows), by_chip.reshape(-1, 2 * rows)

    def joined(*blocks):
        return jnp.concatenate(blocks)

    def relayed(block, vertical):
        return jnp.where(diagonal, vertical, block)

    def plane_weights(*blocks):
        halves = [
            jnp.concatenate([jnp.where(diagonal, block, vertical), horizontal], axis=1)
            for block, vertical, horizontal in (blocks[:3], blocks[3:])
        ]
        return jnp.concatenate(halves)

    def stacked(*news):
        return tuple(jnp.stack(news[i::3], axis=1)[None] for i in range(3))

    def slot_product(slot_rows, left, right):
        total = jnp.dot(slot_rows[:, :rows], left, preferred_element_type=F32)
        total += jnp.dot(slot_rows[:, rows:], right, preferred_element_type=F32)
        keep, give = jnp.split(total, 2)
        return give.astype(BF16), keep

    def folded(kept, got):
        keep, give = jnp.split(kept + got.astype(F32), 2)
        return give.astype(BF16), keep

    def activate(*parts):
        sums = [kept + got.astype(F32) for kept, got in zip(parts[::2], parts[1::2])]
        up = jnp.concatenate(sums[1:], axis=1)
        return (jax.nn.silu(sums[0]) * up).astype(BF16)

    def down_product(left, right, near, far):
        slots = jnp.concatenate([left, right], axis=1)
        down = jnp.concatenate([near, far])
        return lax.dot_general(slots, down, BY_LAST, preferred_element_type=F32).astype(BF16)

    (cot_give,) = mark(give(far_first, 1)(learn_cot))
    cot_got = send("cot_got", cot_give, "fsdp", CORES)
    act = mark(activated(preact, hidden_cot))
    act_got = send("act_got", act, "fsdp", CORES)
    (d_gb,) = mark(token_sums((3,), whole, (BF16,))(learn_cot, cot_got, act, act_got))
    d_b = send("d_b", d_gb, "fsdp", NEAR)
    place, weight = mark(slots(routes, route_weight))
    picked = mark(pick(place, rollout_in))
    picked_far = mark(far_rows(picked))
    there = send("there", picked_far, "fsdp", FAR)
    (in_give,) = mark(give(far_first, 1)(learn_in))
    in_got = send("in_got", in_give, "fsdp", CORES)
    gate, up = mark(pre_grads(preact, hidden_cot))
    gate_got = send("gate_got", gate, "fsdp", CORES)
    up_got = send("up_got", up, "fsdp", CORES)
    g_gb, g_kb = mark(token_sums((3, 1), whole, (BF16, F32))(learn_in, in_got, gate, gate_got))
    d_ga, d_ka = mark(token_sums((2, 0), whole, (BF16, F32))(learn_cot, cot_got, act, act_got))
    d_a = send("d_a", d_ga, "fsdp", NEAR)
    g_b = send("g_b", g_gb, "fsdp", NEAR)
    (d_kb,) = mark(token_sums((1,), whole, (F32,))(learn_cot, cot_got, act, act_got))
    g_ga, g_ka = mark(token_sums((2, 0), whole, (BF16, F32))(learn_in, in_got, gate, gate_got))
    g_a = send("g_a", g_ga, "fsdp", NEAR)
    d_x = mark(given_sum(d_kb, d_b))
    d_across = send("d_across", d_x, "fsdp", FAR)
    g_x = mark(given_sum(g_kb, g_b))
    g_across = send("g_across", g_x, "fsdp", FAR)
    row_give, row_keep = mark(take_rows(picked, there))
    row_got = send("row_got", row_give, "fsdp", CORES)
    u_gb, u_kb = mark(token_sums((3, 1), whole, (BF16, F32))(learn_in, in_got, up, up_got))
    u_b = send("u_b", u_gb, "fsdp", NEAR)
    both = mark(both_cores(row_keep, row_got))
    turned = send("turned", both, ("grp", "tp"), TURN)
    rotated = send("rotated", both, ("grp", "tp"), ROUND)
    d_shard, *d_all = mark(update(2, whole)(d_ka, d_a, d_across))
    d_other = send("d_other", d_shard, "fsdp", FAR)
    vert_z = send("vert_z", d_shard, "grp", SWAP)
    g_shard, *g_all = mark(update(0, whole)(g_ka, g_a, g_across))
    g_near = send("g_near", g_shard, "fsdp", NEAR)
    u_x = mark(given_sum(u_kb, u_b))
    u_across = send("u_across", u_x, "fsdp", FAR)
    u_ga, u_ka = mark(token_sums((2, 0), whole, (BF16, F32))(learn_in, in_got, up, up_got))
    u_a = send("u_a", u_ga, "fsdp", NEAR)
    relay_z = mark(relayed(d_shard, vert_z))
    hori_z = send("hori_z", relay_z, "tp", SWAP)
    slot_rows, slot_rows_g = mark(plane_rows(turned, rotated))
    g_core, g_half = mark(slot_product(slot_rows_g, g_shard, g_near))
    g_core_got = send("g_core_got", g_core, "fsdp", CORES)
    g_far, g_quarter = mark(folded(g_half, g_core_got))
    g_far_got = send("g_far_got", g_far, "fsdp", FAR)
    u_shard, *u_all = mark(update(1, whole)(u_ka, u_a, u_across))
    u_near = send("u_near", u_shard, "fsdp", NEAR)
    d_other = wait(d_other)
    vert_f = send("vert_f", hold(d_other), "grp", SWAP)
    master_new, moment_new, second_new = mark(stacked(*g_all, *u_all, *d_all))
    hori_z = wait(hori_z)
    u_core, u_half = step(slot_product, slot_rows, u_shard, u_near)
    u_core_got = send("u_core_got", u_core, "fsdp", CORES)
    u_grp, u_quarter = step(folded, u_half, u_core_got)
    u_grp_got = send("u_grp_got", u_grp, "grp", SWAP)
    relay_f = step(relayed, d_other, vert_f)
    u_far, u_sum = step(folded, u_quarter, u_grp_got)
    u_far_got = send("u_far_got", u_far, "fsdp", FAR)
    hori_f = send("hori_f", relay_f, "tp", SWAP)
    g_grp, g_sum = step(folded, g_quarter, g_far_got)
    g_grp_got = send("g_grp_got", g_grp, "grp", SWAP)
    down = step(plane_weights, d_shard, vert_z, hori_z, d_other, vert_f, hori_f)
    down_got = send("down_got", down, "fsdp", CORES)
    hidden = mark(activate(g_sum, g_grp_got, u_sum, u_far_got))
    near_hidden = send("near_hidden", hidden, "fsdp", NEAR)
    near_turned = send("near_turned", hidden, ("fsdp", "tp"), NEAR_TURNED)
    beside = send("beside", hidden, "tp", SWAP)
    near_out = mark(down_product(near_hidden, near_turned, down, down_got))
    near_out_got = send("near_out_got", near_out, "fsdp", NEAR)
    out = mark(down_product(hidden, beside, down, down_got))

    slot_out = jnp.concatenate([out, near_out_got], axis=1)
    expert_out = spread(slot_out, place, weight, line)
    return (master_new, moment_new, second_new, expert_out)


def on_device(
    learn_in,
    learn_cot,
    preact,
    hidden_cot,
    master,
    moment,
    second,
    rollout_in,
    routes,
    route_weight,
):
    hidden_width = preact.shape[2]
    hidden_act, grad_gate, grad_up = activations(preact, hidden_cot)
    pre_grads = jnp.concatenate([grad_gate, grad_up], axis=1)
    front = lax.dot_general(
        learn_in, pre_grads, BY_TOKENS, preferred_element_type=F32
    ).reshape(master.shape[1] * lax.axis_size("fsdp"), 2, hidden_width)
    back = lax.dot_general(learn_cot, hidden_act, BY_TOKENS, preferred_element_type=F32)[:, None, :]
    grad = lax.psum_scatter(
        jnp.concatenate([front, back], axis=1).astype(BF16),
        "fsdp",
        scatter_dimension=0,
        tiled=True,
    ).astype(F32)[None]
    master_new, moment_new, second_new = adam(master, moment, second, grad)
    half_rows = lax.all_gather(master_new.astype(BF16), "fsdp", axis=1, tiled=True)
    passed = lax.all_gather(half_rows, "grp", axis=0, tiled=True).reshape(-1, 3, hidden_width)
    weight_in = passed[:, :2, :].reshape(-1, 2 * hidden_width)
    place, weight = slots(routes, route_weight)
    slot_rows = lax.all_gather(pick(place, rollout_in), "tp", axis=1, tiled=True)
    slot_pre = jnp.dot(slot_rows, weight_in, preferred_element_type=F32)
    slot_hidden = jax.nn.silu(slot_pre[:, :hidden_width]) * slot_pre[:, hidden_width:]
    partial_out = lax.dot_general(
        slot_hidden.astype(BF16), passed[:, 2, :], BY_LAST, preferred_element_type=F32
    )
    slot_out = lax.psum_scatter(
        partial_out.astype(BF16), "tp", scatter_dimension=1, tiled=True
    )
    placed = jnp.dot(place, slot_out, preferred_element_type=F32)
    expert_out = (weight * placed).astype(BF16)
    return (master_new, moment_new, second_new, expert_out)


def solution(mesh):
    in_specs = (
        P("fsdp", "grp"),
        P("fsdp", "grp"),
        P("fsdp", None, "tp"),
        P("fsdp", "tp"),
        P("grp", "fsdp", None, "tp"),
        P("grp", "fsdp", None, "tp"),
        P("grp", "fsdp", None, "tp"),
        P(("fsdp", "grp"), "tp"),
        P(("fsdp", "grp"), None),
        P(("fsdp", "grp"), None),
    )
    out_specs = (
        P("grp", "fsdp", None, "tp"),
        P("grp", "fsdp", None, "tp"),
        P("grp", "fsdp", None, "tp"),
        P(("fsdp", "grp"), "tp"),
    )
    small = (mesh.shape["fsdp"], mesh.shape["grp"], mesh.shape["tp"]) == (8, 2, 2)
    return jax.shard_map(
        on_line if small else on_device,
        mesh=mesh,
        in_specs=in_specs,
        out_specs=out_specs,
        check_vma=False,
    )
```
